32 devices in a mesh: elem: 8 (over z, y), col: 4 (over x, core).
Axes of the slice: x: 2, y: 2, z: 4, core: 2. Of those that a mesh axis runs over, the one named last changes fastest.
Arguments:
- gas: float32 [6, 93, 32768], P(None, None, ('elem', 'col')), may hold values from 0.01 to 0.3
- layer_mass: float32 [93, 32768], P(None, ('elem', 'col')), may hold values from 0.5 to 2
- solar_zenith_cosine: float32 [32768], P(('elem', 'col')), may hold values from 0.1 to 1
- albedo: float32 [32768], P(('elem', 'col')), may hold values from 0.05 to 0.6
- span_map: int32 [32768], P(('elem', 'col')), may hold values from 0 to 1023, as said below
- cloud: float32 [14, 93, 32768], P(None, None, ('elem', 'col')), may hold values from 0.001 to 0.03
- sunlit: int32 [32768], P(('elem', 'col')), may hold values from 0 to 1, as said below
- kabs: float32 [56, 6], replicated, may hold values from 0.002 to 0.02
- solar: float32 [56], replicated, may hold values from 0.1 to 1
Outputs:
- heating: float32 [93, 32768], P(None, ('elem', 'col'))
The draws below stay inside these ranges and needn't reach their ends.
Inputs may be any that keep to these rules, and one draw needn't show every extreme that they name: `span_map`: within each device's 1024 consecutive entries the values are a permutation of 0 to 1023. 1 marks a sunlit column; the device at elem index e and the device at elem index e + 8 / 2 (modulo 8, same col index) hold exactly 1024 sunlit columns together, and in every draw some device has all of its 1024 columns sunlit.
All inputs are finite; a program needn't handle non-finite values.
Results may differ from the reference program's by a relative error of at most 0.0003.
Values sent between devices are 32-bit elements; how exact they have to be, the bound alone decides.
A program may use at most 128 MiB of HBM per device.

```python
import math
import jax
import jax.numpy as jnp
from jax import lax

GAS = 6
BANDS = 14
LEV = 93
COLS = 1024
G = 56
COLUMNS = 32768
SLOTS = 32
GROUPS = 8


def draw_span_map(key, part):
    keys = jax.random.split(jax.random.fold_in(key, 11), COLUMNS // COLS)
    perms = jax.vmap(lambda one_key: jax.random.permutation(one_key, COLS))(keys)
    return perms.reshape(-1).astype(jnp.int32)


def draw_sunlit(key, part):
    devices = COLUMNS // COLS
    inner = devices // GROUPS
    half = GROUPS // 2
    pair_total = half * inner
    day_counts = jax.random.randint(jax.random.fold_in(key, 23), (pair_total,), COLS // 2, COLS + 1)
    full_pair = jax.random.randint(jax.random.fold_in(key, 29), (), 0, pair_total)
    pair_index = jnp.arange(pair_total, dtype=jnp.int32)
    day_counts = jnp.where(pair_index == full_pair, COLS, day_counts).astype(jnp.int32)
    day_side = jax.random.randint(jax.random.fold_in(key, 31), (pair_total,), 0, 2)
    device = jnp.arange(devices, dtype=jnp.int32)
    group = device // inner
    lane = device % inner
    pair_of = group % half * inner + lane
    upper = group // half
    count = jnp.where(upper == day_side[pair_of], day_counts[pair_of], COLS - day_counts[pair_of]).astype(jnp.int32)
    keys = jax.random.split(jax.random.fold_in(key, 37), devices)
    ranks = jax.vmap(lambda one_key: jax.random.permutation(one_key, COLS))(keys).astype(jnp.int32)
    return (ranks < count[:, None]).astype(jnp.int32).reshape(-1)


def shard_levels(own_key, dims, cuts, smallest, largest):
    loudness, own = 1.0, jax.random.fold_in(own_key, 6)
    for position, parts in cuts:
        steps = jnp.exp(jax.random.uniform(jax.random.fold_in(own, position), (parts,), jnp.float32, smallest / len(cuts), largest / len(cuts)))
        loudness = loudness * jnp.repeat(steps, dims[position] // parts).reshape([-1 if axis == position else 1 for axis in range(len(dims))])
    return loudness


def setup_inputs(seed: int = 0) -> dict:
    seeds = jax.random.split(jax.random.key(seed), 10)
    return {
        "gas": jnp.clip(jnp.exp(math.log(0.3) - 3.4011974 * jax.random.uniform(seeds[0], (GAS, LEV, COLUMNS), jnp.float32) ** shard_levels(seeds[0], (GAS, LEV, COLUMNS), ((2, 32),), -0.2, 0.2)), 0.01, 0.3),
        "layer_mass": jnp.clip(jnp.exp(math.log(2.0) - 1.3862944 * jax.random.uniform(seeds[1], (LEV, COLUMNS), jnp.float32) ** shard_levels(seeds[1], (LEV, COLUMNS), ((1, 32),), -0.2, 0.2)), 0.5, 2.0),
        "solar_zenith_cosine": jnp.clip(0.1 + 0.9 * jax.random.uniform(seeds[2], (COLUMNS,), jnp.float32) ** shard_levels(seeds[2], (COLUMNS,), ((0, 32),), -0.2, 0.2), 0.1, 1.0),
        "albedo": jnp.clip(0.05 + 0.55 * jax.random.uniform(seeds[3], (COLUMNS,), jnp.float32) ** shard_levels(seeds[3], (COLUMNS,), ((0, 32),), -0.2, 0.2), 0.05, 0.6),
        "span_map": draw_span_map(jax.random.fold_in(seeds[9], 71), 0),
        "cloud": jnp.clip(jnp.exp(math.log(0.03) - 3.4011973 * jax.random.uniform(seeds[5], (BANDS, LEV, COLUMNS), jnp.float32) ** shard_levels(seeds[5], (BANDS, LEV, COLUMNS), ((2, 32),), -0.2, 0.2)), 0.001, 0.03),
        "sunlit": draw_sunlit(jax.random.fold_in(seeds[9], 71), 0),
        "kabs": jnp.clip(jnp.exp(jax.random.uniform(seeds[7], (G, GAS), jnp.float32, math.log(0.002), math.log(0.02))), 0.002, 0.02),
        "solar": jnp.clip(jnp.exp(jax.random.uniform(seeds[8], (G,), jnp.float32, math.log(0.1), math.log(1.0))), 0.1, 1.0),
    }


def shortwave(absorber_block, cloud_block, mass_block, zenith, surface, kabs, solar):
    gpoints = kabs.shape[0]
    optical_thickness = jnp.einsum("bw,wev->bev", kabs, absorber_block, precision=lax.Precision.HIGHEST)
    optical_thickness = optical_thickness + jnp.repeat(cloud_block, gpoints // cloud_block.shape[0], axis=0)
    depth = jnp.cumsum(optical_thickness, axis=1)
    depth = jnp.concatenate([jnp.zeros((gpoints, 1, depth.shape[2]), jnp.float32), depth], axis=1)
    down = solar[:, None, None] * zenith[None, None, :] * jnp.exp(-depth / zenith[None, None, :])
    total_depth = depth[:, -1:, :]
    upward = surface[None, None, :] * down[:, -1:, :] * jnp.exp(-1.66 * (total_depth - depth))
    net_flux = down - upward
    absorbed = jnp.sum(net_flux[:, :-1, :] - net_flux[:, 1:, :], axis=0)
    return absorbed / mass_block


def reference(gas, layer_mass, solar_zenith_cosine, albedo, span_map, cloud, sunlit, kabs, solar):
    column_index = jnp.arange(COLUMNS, dtype=jnp.int32)
    owner = column_index // COLS
    target = (span_map // SLOTS) * COLS + owner * SLOTS + span_map % SLOTS
    cloud_here = cloud[:, :, target]
    lit_here = sunlit[target]

    def one_block(block_index):
        start = (block_index * COLS).astype(jnp.int32)
        absorber_block = lax.dynamic_slice_in_dim(gas, start, COLS, 2)
        cloud_block = lax.dynamic_slice_in_dim(cloud_here, start, COLS, 2)
        mass_block = lax.dynamic_slice_in_dim(layer_mass, start, COLS, 1)
        zenith = lax.dynamic_slice_in_dim(solar_zenith_cosine, start, COLS, 0)
        surface = lax.dynamic_slice_in_dim(albedo, start, COLS, 0)
        daylit_block = lax.dynamic_slice_in_dim(lit_here, start, COLS, 0)
        rates = shortwave(absorber_block, cloud_block, mass_block, zenith, surface, kabs, solar)
        return jnp.where(daylit_block[None, :] == 1, rates, jnp.zeros_like(rates))

    column_blocks = lax.map(one_block, jnp.arange(COLUMNS // COLS, dtype=jnp.int32))
    return jnp.transpose(column_blocks, (1, 0, 2)).reshape(LEV, COLUMNS)
```

```python
import functools

import jax
import jax.numpy as jnp
from jax import lax
from jax.experimental import pallas as pl
from jax.experimental.pallas import tpu as pltpu
from jax.sharding import PartitionSpec as P

MESH = pl.DeviceIdType.MESH
LANES = 128
LOG2E = 1.4426950408889634


def flip(a, b, size):
    out, bit = 0, 1
    while bit < size:
        out = out + lax.rem(lax.div(a, bit) + lax.div(b, bit), 2) * bit
        bit *= 2
    return out


def swap_blocks(rows, blocks, slots):
    lane = lax.broadcasted_iota(jnp.int32, rows[0].shape, 1) // slots
    out = []
    for b in range(blocks):
        piece = None
        for a in range(blocks):
            shift = (a - b) * slots % LANES
            moved = pltpu.roll(rows[a], shift, 1) if shift else rows[a]
            piece = moved if piece is None else jnp.where(lane == a, moved, piece)
        out.append(piece)
    return out


def split_two(x):
    high = x.astype(jnp.bfloat16)
    return high, (x - high.astype(jnp.float32)).astype(jnp.bfloat16)


def fused_kernel(
    sizes,
    gas_hbm, cloud_hbm, zenith_ref, albedo_ref, span_ref, lit_ref, kabs_ref, solar_ref,
    out_ref,
    gas_v, cloud_v, high_v, low_v, onehot, sends, recvs, stack, cums, rates_out, rates_in, total,
    gas_sem, cloud_sem, send_sem, recv_sem, rate_send_sem, rate_recv_sem,
):
    gases, levels, bands, per_band, devices, cols, slots, part, send_order, work_order = sizes
    blocks = LANES // slots
    full = part * blocks
    tiles = devices // blocks
    width = tiles * LANES
    me = lax.axis_index("elem") * cols + lax.axis_index("col")
    mine, place = lax.div(me, blocks), lax.rem(me, blocks)

    def at(device):
        return (lax.div(device, cols), lax.rem(device, cols))

    gas_copy = pltpu.make_async_copy(gas_hbm, gas_v, gas_sem)
    gas_copy.start()
    cloud_copy = pltpu.make_async_copy(cloud_hbm, cloud_v, cloud_sem)
    cloud_copy.start()

    barrier = pltpu.get_barrier_semaphore()

    def greet(k, carry):
        other = lax.rem(me + k, devices)
        pl.semaphore_signal(
            barrier, inc=1, device_id=at(other), device_id_type=MESH
        )
        return carry

    lax.fori_loop(1, devices, greet, 0)

    def hot(q, carry):
        first = pl.multiple_of(q * LANES, LANES)
        slot = lax.broadcasted_iota(jnp.int32, (LANES, width), 0) + first
        onehot[pl.ds(first, LANES), :] = (slot == span_ref[...]).astype(jnp.float32).astype(jnp.bfloat16)
        return carry

    lax.fori_loop(0, tiles, hot, 0)
    gas_copy.wait()
    for s in range(gases):
        if s == 0:
            tail = [zenith_ref[...], albedo_ref[...], jnp.zeros((full - levels - 2, width), jnp.float32)]
        else:
            tail = [jnp.zeros((full - levels, width), jnp.float32)]
        high, low = split_two(jnp.concatenate([gas_v[s]] + tail, axis=0))
        high_v[s * full : (s + 1) * full, :] = high
        low_v[s * full : (s + 1) * full, :] = low
    pl.semaphore_wait(barrier, devices - 1)

    def state_copy(src, dst, device, sent, came):
        return pltpu.make_async_remote_copy(
            sends.at[src], recvs.at[dst], send_sem.at[sent], recv_sem.at[came],
            device_id=at(device), device_id_type=MESH,
        )

    def rate_copy(src, dst, device, sent, came):
        return pltpu.make_async_remote_copy(
            rates_out.at[src], rates_in.at[dst], rate_send_sem.at[sent], rate_recv_sem.at[came],
            device_id=at(device), device_id_type=MESH,
        )

    def send_tile(k, carry):
        turn = send_order(k)
        q = flip(mine, turn, tiles)
        hot_q = onehot[pl.ds(pl.multiple_of(q * LANES, LANES), LANES), :]
        dims = (((1,), (1,)), ((), ()))
        slotted = lax.dot_general(high_v[...], hot_q, dims, preferred_element_type=jnp.float32)
        slotted = slotted + lax.dot_general(low_v[...], hot_q, dims, preferred_element_type=jnp.float32)
        for s in range(gases):
            rows = [slotted[s * full + j * part : s * full + (j + 1) * part] for j in range(blocks)]
            for t, piece in enumerate(swap_blocks(rows, blocks, slots)):
                sends[q * blocks + t, s * part : (s + 1) * part, :] = piece
        for step in range(blocks):
            t = lax.rem(place + step, blocks)
            to = q * blocks + t

            @pl.when(to != me)
            def _():
                state_copy(to, me, to, to, me).start()

            @pl.when(to == me)
            def _():
                recvs[me] = sends[me]

        return carry

    lax.fori_loop(0, tiles, send_tile, 0)

    stack[levels:full, :] = jnp.zeros((full - levels, stack.shape[1]), jnp.float32)
    upper = lax.broadcasted_iota(jnp.int32, (full, full), 0)
    lower = lax.broadcasted_iota(jnp.int32, (full, full), 1)
    above = (lower < upper).astype(jnp.float32).astype(jnp.bfloat16)
    cloud_copy.wait()

    def work_tile(k, carry):
        turn = work_order(k)
        q = flip(mine, turn, tiles)
        lanes = pl.ds(pl.multiple_of(q * LANES, LANES), LANES)
        for b in range(bands):
            stack[0:levels, (gases + b) * LANES : (gases + b + 1) * LANES] = cloud_v[b, :, lanes]
        for t in range(blocks):
            source = q * blocks + t

            @pl.when(source != me)
            def _():
                state_copy(source, source, source, source, source).wait_recv()

        zenith = surface = None
        for s in range(gases):
            rows = [recvs[q * blocks + t, s * part : (s + 1) * part, :] for t in range(blocks)]
            pieces = swap_blocks(rows, blocks, slots)
            for j, piece in enumerate(pieces):
                keep = max(0, min(part, levels - j * part))
                if keep == 0:
                    continue
                stack[j * part : j * part + keep, s * LANES : (s + 1) * LANES] = piece[0:keep]
            if s == 0:
                row = levels % part
                zenith = pieces[levels // part][row : row + 1]
                row = (levels + 1) % part
                surface = pieces[(levels + 1) // part][row : row + 1]
        for f in range(gases + bands):
            high, low = split_two(stack[:, f * LANES : (f + 1) * LANES])
            cums[f] = jnp.dot(above, high, preferred_element_type=jnp.float32) + jnp.dot(
                above, low, preferred_element_type=jnp.float32
            )
        slant = -LOG2E / zenith

        def band(b, net):
            clouds = cums[gases + b]
            for i in range(per_band):
                g = b * per_band + i
                depth = clouds
                for s in range(gases):
                    depth = depth + kabs_ref[g * gases + s] * cums[s]
                down = jnp.exp2(depth * slant)
                up = jnp.exp2((depth - depth[levels : levels + 1]) * (1.66 * LOG2E))
                net = net + solar_ref[g] * (down - (surface * down[levels : levels + 1]) * up)
            return net

        net = lax.fori_loop(0, bands, band, jnp.zeros((full, LANES), jnp.float32))
        absorbed = (net - pltpu.roll(net, full - 1, 0)) * zenith
        absorbed = jnp.where(lit_ref[:, lanes] == 1, absorbed, jnp.zeros_like(absorbed))
        rows = [absorbed[j * part : (j + 1) * part] for j in range(blocks)]
        for t, piece in enumerate(swap_blocks(rows, blocks, slots)):
            rates_out[q * blocks + t] = piece
        for t in range(blocks):
            to = q * blocks + t

            @pl.when(to != me)
            def _():
                rate_copy(to, me, to, to, me).start()

            @pl.when(to == me)
            def _():
                rates_in[me] = rates_out[me]

        return carry

    lax.fori_loop(0, tiles, work_tile, 0)

    total[...] = jnp.zeros_like(total)

    def gather_tile(k, carry):
        q = flip(mine, work_order(k), tiles)
        for t in range(blocks):
            source = q * blocks + t

            @pl.when(source != me)
            def _():
                rate_copy(source, source, source, source, source).wait_recv()

        rows = [rates_in[q * blocks + t] for t in range(blocks)]
        high, low = split_two(jnp.concatenate(swap_blocks(rows, blocks, slots), axis=0))
        hot_q = onehot[pl.ds(pl.multiple_of(q * LANES, LANES), LANES), :]
        total[...] += jnp.dot(high, hot_q, preferred_element_type=jnp.float32) + jnp.dot(
            low, hot_q, preferred_element_type=jnp.float32
        )
        return carry

    lax.fori_loop(0, tiles, gather_tile, 0)
    out_ref[...] = total[0:levels, :]

    def drain(k, carry):
        other = lax.rem(me + k, devices)
        state_copy(other, me, other, other, me).wait_send()
        rate_copy(other, me, other, other, me).wait_send()
        return carry

    lax.fori_loop(1, devices, drain, 0)


def send_order(k):
    return lax.rem(k + 4, 8)


def work_order(k):
    return k


def fused(elems, cols, gas, layer_mass, solar_zenith_cosine, albedo, span_map, cloud, sunlit, kabs, solar):
    gases, levels, width = gas.shape
    bands = cloud.shape[0]
    gpoints = kabs.shape[0]
    devices = elems * cols
    slots = width // devices
    blocks = LANES // slots
    part = -(-(levels + 2) // (8 * blocks)) * 8
    full = part * blocks
    sizes = (gases, levels, bands, gpoints // bands, devices, cols, slots, part, send_order, work_order)
    vmem = pl.BlockSpec(memory_space=pltpu.VMEM)
    smem = pl.BlockSpec(memory_space=pltpu.SMEM)
    hbm = pl.BlockSpec(memory_space=pl.ANY)
    f32, bf16 = jnp.float32, jnp.bfloat16
    absorbed = pl.pallas_call(
        functools.partial(fused_kernel, sizes),
        out_shape=jax.ShapeDtypeStruct((levels, width), f32),
        in_specs=[hbm, hbm, vmem, vmem, vmem, vmem, smem, smem],
        out_specs=vmem,
        scratch_shapes=[
            pltpu.VMEM((gases, levels, width), f32),
            pltpu.VMEM((bands, levels, width), f32),
            pltpu.VMEM((gases * full, width), bf16),
            pltpu.VMEM((gases * full, width), bf16),
            pltpu.VMEM((width, width), bf16),
            pltpu.VMEM((devices, gases * part, LANES), f32),
            pltpu.VMEM((devices, gases * part, LANES), f32),
            pltpu.VMEM((full, (gases + bands) * LANES), f32),
            pltpu.VMEM((gases + bands, full, LANES), f32),
            pltpu.VMEM((devices, part, LANES), f32),
            pltpu.VMEM((devices, part, LANES), f32),
            pltpu.VMEM((full, width), f32),
            pltpu.SemaphoreType.DMA,
            pltpu.SemaphoreType.DMA,
            pltpu.SemaphoreType.DMA((devices,)),
            pltpu.SemaphoreType.DMA((devices,)),
            pltpu.SemaphoreType.DMA((devices,)),
            pltpu.SemaphoreType.DMA((devices,)),
        ],
        compiler_params=pltpu.CompilerParams(
            collective_id=0, has_side_effects=True, vmem_limit_bytes=40 * 1024 * 1024
        ),
        name="remap_and_radiate",
    )(
        gas, cloud, solar_zenith_cosine[None, :], albedo[None, :], span_map[None, :], sunlit[None, :],
        kabs.reshape(-1), solar,
    )
    return absorbed / layer_mass


def solution(mesh):
    in_specs = (
        P(None, None, ("elem", "col")),
        P(None, ("elem", "col")),
        P(("elem", "col")),
        P(("elem", "col")),
        P(("elem", "col")),
        P(None, None, ("elem", "col")),
        P(("elem", "col")),
        P(),
        P(),
    )
    out_specs = P(None, ("elem", "col"))
    body = functools.partial(fused, mesh.shape["elem"], mesh.shape["col"])
    return jax.shard_map(
        body, mesh=mesh, in_specs=in_specs, out_specs=out_specs, check_vma=False
    )
```

```python
import functools

import jax
import jax.numpy as jnp
from jax import lax
from jax.experimental import pallas as pl
from jax.experimental.pallas import tpu as pltpu
from jax.sharding import PartitionSpec as P

MESH = pl.DeviceIdType.MESH
LANES = 128
LOG2E = 1.4426950408889634


def flip(a, b, size):
    out, bit = 0, 1
    while bit < size:
        out = out + lax.rem(lax.div(a, bit) + lax.div(b, bit), 2) * bit
        bit *= 2
    return out


def swap_blocks(rows, blocks, slots):
    lane = lax.broadcasted_iota(jnp.int32, rows[0].shape, 1) // slots
    out = []
    for b in range(blocks):
        piece = None
        for a in range(blocks):
            shift = (a - b) * slots % LANES
            moved = pltpu.roll(rows[a], shift, 1) if shift else rows[a]
            piece = moved if piece is None else jnp.where(lane == a, moved, piece)
        out.append(piece)
    return out


def split_two(x):
    high = x.astype(jnp.bfloat16)
    return high, (x - high.astype(jnp.float32)).astype(jnp.bfloat16)


def fused_kernel(
    sizes,
    gas_hbm, cloud_hbm, zenith_ref, albedo_ref, span_ref, lit_ref, kabs_ref, solar_ref,
    out_ref,
    gas_v, cloud_v, high_v, low_v, onehot, sends, recvs, stack, cums, rates_out, rates_in, total,
    gas_sem, cloud_sem, send_sem, recv_sem, rate_send_sem, rate_recv_sem,
):
    gases, levels, bands, per_band, devices, cols, slots, part, send_order, work_order = sizes
    blocks = LANES // slots
    full = part * blocks
    tiles = devices // blocks
    width = tiles * LANES
    me = lax.axis_index("elem") * cols + lax.axis_index("col")
    mine, place = lax.div(me, blocks), lax.rem(me, blocks)

    def at(device):
        return (lax.div(device, cols), lax.rem(device, cols))

    gas_copy = pltpu.make_async_copy(gas_hbm, gas_v, gas_sem)
    gas_copy.start()
    cloud_copy = pltpu.make_async_copy(cloud_hbm, cloud_v, cloud_sem)
    cloud_copy.start()

    barrier = pltpu.get_barrier_semaphore()

    def greet(k, carry):
        other = lax.rem(me + k, devices)
        pl.semaphore_signal(
            barrier, inc=1, device_id=at(other), device_id_type=MESH
        )
        return carry

    lax.fori_loop(1, devices, greet, 0)

    def hot(q, carry):
        first = pl.multiple_of(q * LANES, LANES)
        slot = lax.broadcasted_iota(jnp.int32, (LANES, width), 0) + first
        onehot[pl.ds(first, LANES), :] = (slot == span_ref[...]).astype(jnp.float32).astype(jnp.bfloat16)
        return carry

    lax.fori_loop(0, tiles, hot, 0)
    gas_copy.wait()
    for s in range(gases):
        if s == 0:
            tail = [zenith_ref[...], albedo_ref[...], jnp.zeros((full - levels - 2, width), jnp.float32)]
        else:
            tail = [jnp.zeros((full - levels, width), jnp.float32)]
        high, low = split_two(jnp.concatenate([gas_v[s]] + tail, axis=0))
        high_v[s * full : (s + 1) * full, :] = high
        low_v[s * full : (s + 1) * full, :] = low
    pl.semaphore_wait(barrier, devices - 1)

    def state_copy(src, dst, device, sent, came):
        return pltpu.make_async_remote_copy(
            sends.at[src], recvs.at[dst], send_sem.at[sent], recv_sem.at[came],
            device_id=at(device), device_id_type=MESH,
        )

    def rate_copy(src, dst, device, sent, came):
        return pltpu.make_async_remote_copy(
            rates_out.at[src], rates_in.at[dst], rate_send_sem.at[sent], rate_recv_sem.at[came],
            device_id=at(device), device_id_type=MESH,
        )

    def send_tile(k, carry):
        turn = send_order(k)
        q = flip(mine, turn, tiles)
        hot_q = onehot[pl.ds(pl.multiple_of(q * LANES, LANES), LANES), :]
        dims = (((1,), (1,)), ((), ()))
        slotted = lax.dot_general(high_v[...], hot_q, dims, preferred_element_type=jnp.float32)
        slotted = slotted + lax.dot_general(low_v[...], hot_q, dims, preferred_element_type=jnp.float32)
        for s in range(gases):
            rows = [slotted[s * full + j * part : s * full + (j + 1) * part] for j in range(blocks)]
            for t, piece in enumerate(swap_blocks(rows, blocks, slots)):
                sends[q * blocks + t, s * part : (s + 1) * part, :] = piece
        for step in range(blocks):
            t = lax.rem(place + step, blocks)
            to = q * blocks + t

            @pl.when(to != me)
            def _():
                state_copy(to, me, to, to, me).start()

            @pl.when(to == me)
            def _():
                recvs[me] = sends[me]

        return carry

    lax.fori_loop(0, tiles, send_tile, 0)

    stack[levels:full, :] = jnp.zeros((full - levels, stack.shape[1]), jnp.float32)
    upper = lax.broadcasted_iota(jnp.int32, (full, full), 0)
    lower = lax.broadcasted_iota(jnp.int32, (full, full), 1)
    above = (lower < upper).astype(jnp.float32).astype(jnp.bfloat16)
    cloud_copy.wait()

    total[...] = jnp.zeros_like(total)

    def gather_tile(k, carry):
        q = flip(mine, work_order(k), tiles)
        for t in range(blocks):
            source = q * blocks + t

            @pl.when(source != me)
            def _():
                rate_copy(source, source, source, source, source).wait_recv()

        rows = [rates_in[q * blocks + t] for t in range(blocks)]
        high, low = split_two(jnp.concatenate(swap_blocks(rows, blocks, slots), axis=0))
        hot_q = onehot[pl.ds(pl.multiple_of(q * LANES, LANES), LANES), :]
        total[...] += jnp.dot(high, hot_q, preferred_element_type=jnp.float32) + jnp.dot(
            low, hot_q, preferred_element_type=jnp.float32
        )
        return carry

    def work_tile(k, carry):
        turn = work_order(k)
        q = flip(mine, turn, tiles)
        lanes = pl.ds(pl.multiple_of(q * LANES, LANES), LANES)
        for b in range(bands):
            stack[0:levels, (gases + b) * LANES : (gases + b + 1) * LANES] = cloud_v[b, :, lanes]
        for t in range(blocks):
            source = q * blocks + t

            @pl.when(source != me)
            def _():
                state_copy(source, source, source, source, source).wait_recv()

        zenith = surface = None
        for s in range(gases):
            rows = [recvs[q * blocks + t, s * part : (s + 1) * part, :] for t in range(blocks)]
            pieces = swap_blocks(rows, blocks, slots)
            for j, piece in enumerate(pieces):
                keep = max(0, min(part, levels - j * part))
                if keep == 0:
                    continue
                stack[j * part : j * part + keep, s * LANES : (s + 1) * LANES] = piece[0:keep]
            if s == 0:
                row = levels % part
                zenith = pieces[levels // part][row : row + 1]
                row = (levels + 1) % part
                surface = pieces[(levels + 1) // part][row : row + 1]
        for f in range(gases + bands):
            high, low = split_two(stack[:, f * LANES : (f + 1) * LANES])
            summed = jnp.dot(above, high, preferred_element_type=jnp.float32) + jnp.dot(
                above, low, preferred_element_type=jnp.float32
            )
            cums[f] = summed * (1.66 * LOG2E)
        slant = -1.0 / (1.66 * zenith)

        def band(b, net):
            clouds = cums[gases + b]
            for i in range(per_band):
                g = b * per_band + i
                depth = clouds
                for s in range(gases):
                    depth = depth + kabs_ref[g * gases + s] * cums[s]
                down = jnp.exp2(depth * slant)
                up = jnp.exp2(depth)
                back = surface * down[levels : levels + 1] * jnp.exp2(-depth[levels : levels + 1])
                net = net + solar_ref[g] * (down - back * up)
            return net

        net = lax.fori_loop(0, bands, band, jnp.zeros((full, LANES), jnp.float32))
        absorbed = (net - pltpu.roll(net, full - 1, 0)) * zenith
        absorbed = jnp.where(lit_ref[:, lanes] == 1, absorbed, jnp.zeros_like(absorbed))
        rows = [absorbed[j * part : (j + 1) * part] for j in range(blocks)]
        for t, piece in enumerate(swap_blocks(rows, blocks, slots)):
            rates_out[q * blocks + t] = piece
        for t in range(blocks):
            to = q * blocks + t

            @pl.when(to != me)
            def _():
                rate_copy(to, me, to, to, me).start()

            @pl.when(to == me)
            def _():
                rates_in[me] = rates_out[me]

        return carry

    lax.fori_loop(0, tiles, work_tile, 0)
    lax.fori_loop(0, tiles, gather_tile, 0)
    out_ref[...] = total[0:levels, :]

    def drain(k, carry):
        other = lax.rem(me + k, devices)
        state_copy(other, me, other, other, me).wait_send()
        rate_copy(other, me, other, other, me).wait_send()
        return carry

    lax.fori_loop(1, devices, drain, 0)


def send_order(k):
    return lax.rem(k + 1, 2) * 4 + lax.div(k, 2)


def work_order(k):
    return lax.rem(k, 2) * 4 + lax.div(k, 2)


def fused(elems, cols, gas, layer_mass, solar_zenith_cosine, albedo, span_map, cloud, sunlit, kabs, solar):
    gases, levels, width = gas.shape
    bands = cloud.shape[0]
    gpoints = kabs.shape[0]
    devices = elems * cols
    slots = width // devices
    blocks = LANES // slots
    part = -(-(levels + 2) // (8 * blocks)) * 8
    full = part * blocks
    sizes = (gases, levels, bands, gpoints // bands, devices, cols, slots, part, send_order, work_order)
    vmem = pl.BlockSpec(memory_space=pltpu.VMEM)
    smem = pl.BlockSpec(memory_space=pltpu.SMEM)
    hbm = pl.BlockSpec(memory_space=pltpu.HBM)
    f32, bf16 = jnp.float32, jnp.bfloat16
    absorbed = pl.pallas_call(
        functools.partial(fused_kernel, sizes),
        out_shape=jax.ShapeDtypeStruct((levels, width), f32),
        in_specs=[hbm, hbm, vmem, vmem, vmem, vmem, smem, smem],
        out_specs=vmem,
        scratch_shapes=[
            pltpu.VMEM((gases, levels, width), f32),
            pltpu.VMEM((bands, levels, width), f32),
            pltpu.VMEM((gases * full, width), bf16),
            pltpu.VMEM((gases * full, width), bf16),
            pltpu.VMEM((width, width), bf16),
            pltpu.VMEM((devices, gases * part, LANES), f32),
            pltpu.VMEM((devices, gases * part, LANES), f32),
            pltpu.VMEM((full, (gases + bands) * LANES), f32),
            pltpu.VMEM((gases + bands, full, LANES), f32),
            pltpu.VMEM((devices, part, LANES), f32),
            pltpu.VMEM((devices, part, LANES), f32),
            pltpu.VMEM((full, width), f32),
            pltpu.SemaphoreType.DMA,
            pltpu.SemaphoreType.DMA,
            pltpu.SemaphoreType.DMA((devices,)),
            pltpu.SemaphoreType.DMA((devices,)),
            pltpu.SemaphoreType.DMA((devices,)),
            pltpu.SemaphoreType.DMA((devices,)),
        ],
        compiler_params=pltpu.CompilerParams(
            collective_id=0, has_side_effects=True, vmem_limit_bytes=62 * 1024 * 1024
        ),
        name="remap_and_radiate",
    )(
        gas, cloud, solar_zenith_cosine[None, :], albedo[None, :], span_map[None, :], sunlit[None, :],
        kabs.reshape(-1), solar,
    )
    return absorbed / layer_mass


def solution(mesh):
    in_specs = (
        P(None, None, ("elem", "col")),
        P(None, ("elem", "col")),
        P(("elem", "col")),
        P(("elem", "col")),
        P(("elem", "col")),
        P(None, None, ("elem", "col")),
        P(("elem", "col")),
        P(),
        P(),
    )
    out_specs = P(None, ("elem", "col"))
    body = functools.partial(fused, mesh.shape["elem"], mesh.shape["col"])
    return jax.shard_map(
        body, mesh=mesh, in_specs=in_specs, out_specs=out_specs, check_vma=False
    )
```
